32 devices in a mesh: grp: 4 (over z), seq: 8 (over y, x, core).
Axes of the slice: x: 2, y: 2, z: 4, core: 2. Of those that a mesh axis runs over, the one named last changes fastest.
Arguments:
- tokens: bfloat16 [2048, 2560], P('seq', 'grp'), may hold values from -6 to 6
- cotangent: bfloat16 [2048, 2560], P('seq', 'grp'), may hold values from -3 to 3
- route_ids: int32 [2048, 2], P('seq'), may hold values from 0 to 7, all different within a row; in each aligned block of 256 rows (0 to 255, 256 to 511, ...) at most 96 rows name the same one
- route_weights: bfloat16 [2048, 2], P('seq'), may hold values from 0.099609375 to 1
- reset_steps: int32 [128], P('seq'), may hold values from 0 to 3
- decay: float32 [8, 2048], P('seq', 'grp'), may hold values from 0.2 to 0.9
- w_up: bfloat16 [8, 2560, 2048], P('seq', None, 'grp'), may hold values from -0.15625 to 0.15625
- w_down: bfloat16 [8, 2048, 2560], P('seq', 'grp'), may hold values from -0.125 to 0.125
Outputs:
- grad_x: bfloat16 [2048, 2560], P('seq', 'grp')
- grad_route: float32 [2048, 2], P('seq')
- grad_up: bfloat16 [8, 2560, 2048], P('seq', None, 'grp')
- grad_down: bfloat16 [8, 2048, 2560], P('seq', 'grp')
The draws below stay inside these ranges and needn't reach their ends.
Inputs may be any that keep to these rules, and one draw needn't show every extreme that they name: `route_ids`: each token names two different experts. Within the 256 tokens of one index of seq no expert is named more than 96 times, and in some such blocks an expert is named exactly 96 times.
All inputs are finite; a program needn't handle non-finite values.
Results may differ from the reference program's by a relative error of at most 0.012.
Values may be sent and summed in bfloat16 or wider, within the bound.
A program may use at most 128 MiB of HBM per device.

```python
import math
import jax
import jax.numpy as jnp
import numpy as np
from jax import lax

D = 2560
FF = 2048
STEPS = 4
RB = 16
TOK_DEV = 256
E = 8
CAP = 96
TOKENS = 2048
N_GRP = 4
N_SEQ = 8


def touch_ends(drawn, rng, low, high):
    place = [jax.random.randint(jax.random.fold_in(rng, axis), (), 0, length) for axis, length in enumerate(drawn.shape)]
    longest = drawn.shape.index(max(drawn.shape))
    neighbour = place[:longest] + [(place[longest] + 1) % drawn.shape[longest]] + place[longest + 1:]
    return drawn.at[tuple(place)].set(low).at[tuple(neighbour)].set(high)


def spiked(array, key, source, target, parts, factor):
    owner, partner = [(jnp.arange(array.shape[dim]) // (array.shape[dim] // parts)).reshape([-1 if axis == dim else 1 for axis in range(array.ndim)]) for dim in (source, target)]
    chosen = jax.random.permutation(key, parts)[partner]
    strong = (owner == chosen) | (owner == (partner + parts // 2) % parts)
    return jnp.where(strong, factor * array, array)


def steps_of(rng, shape, cuts, least, top_value):
    level, own = 1.0, jax.random.fold_in(rng, 6)
    for dim, parts in cuts:
        heights = jnp.exp(jax.random.uniform(jax.random.fold_in(own, dim), (parts,), jnp.float32, least / len(cuts), top_value / len(cuts)))
        level = level * jnp.repeat(heights, shape[dim] // parts).reshape([-1 if axis == dim else 1 for axis in range(len(shape))])
    return level


def assign_block(rng, own, number, rows, number_of, top, limit, lean):
    sequence = jax.random.permutation(rng, number_of)
    crowded, ordinary = portions_of(number_of, rows * top, limit, lean, True), portions_of(number_of, rows * top, limit, lean, False)
    places = jnp.arange(number_of)

    def named(lengths, offset_by):
        used = int((lengths > 0).sum())
        fixed = max(1, used // 4)
        passed = fixed + (places - fixed + offset_by * (used - fixed)) % max(1, number_of - fixed)
        return jnp.zeros((number_of,), jnp.int32).at[sequence[jnp.where(places < fixed, places, passed)]].set(jnp.asarray(lengths, jnp.int32))

    lengths = jnp.where(number % 4 == 0, named(crowded, number // 4), named(ordinary, number - number // 4 - 1))
    mixed = jax.random.permutation(jax.random.fold_in(own, 3), number_of)
    giver, receiver = mixed[0:number_of // 2 * 2:2], mixed[1:number_of // 2 * 2:2]
    margin = jnp.minimum(lengths[giver] - 1, limit - lengths[receiver]) // 2
    margin = jnp.where((giver == sequence[0]) | (receiver == sequence[0]) | (lengths[receiver] == 0), 0, jnp.maximum(margin, 0))
    passed = jax.random.randint(jax.random.fold_in(own, 4), (number_of // 2,), 0, 1 << 20) % (margin + 1)
    lengths = lengths.at[giver].add(-passed).at[receiver].add(passed)
    members = jnp.searchsorted(jnp.cumsum(lengths), jnp.arange(rows * top), side="right").astype(jnp.int32)
    grid = members.reshape(top, rows).T
    grid = grid[jax.random.permutation(jax.random.fold_in(own, 1), rows)]
    offset_by = jax.random.randint(jax.random.fold_in(own, 2), (rows, 1), 0, top)
    return jnp.take_along_axis(grid, (jnp.arange(top)[None, :] + offset_by) % top, axis=1)


def portions_of(count, total, most, lean, full):
    loads = [(1 << 20) // math.isqrt(grade ** lean) + 1 for grade in range(1, count + 1)]
    largest = most if full else min(most, max(-(-total // count), total * loads[0] // sum(loads)))
    least = 1 if total - largest >= count - 1 else 0
    holding, rest = [largest] + [least] * (count - 1), total - largest - least * (count - 1)
    while rest > 0:
        candidates = [i for i in range(1, count) if holding[i] < largest] or [i for i in range(1, count) if holding[i] < most]
        pool, left = sum([loads[i] for i in candidates]), rest
        for i in candidates:
            more = min(most - holding[i], max(1, left * loads[i] // pool), rest)
            holding[i] = holding[i] + more
            rest = rest - more
    return np.array(holding)


def bell_draw(rng, extent, width, bound, pieces=(), kind=jnp.bfloat16):
    drawn = jax.random.normal(rng, extent, jnp.float32) * width
    if len(pieces) > 0:
        drawn = steps_of(rng, extent, pieces, -0.22, 0.18) * drawn
    return jnp.clip(drawn, min=-bound, max=bound).astype(kind)


def noise_with(stream_key, shape, width, reach, cuts, heavy, kind=jnp.bfloat16):
    values = width * jax.random.normal(stream_key, shape, jnp.float32)
    if cuts:
        values = values * steps_of(stream_key, shape, cuts, -0.22, 0.18)
    return jnp.clip(spiked(values, jax.random.fold_in(stream_key, 3), *heavy), -reach, reach).astype(kind)


def setup_inputs(seed: int = 0) -> dict:
    arg_keys = jax.random.split(jax.random.key(seed), 9)
    tokens = bell_draw(arg_keys[0], (TOKENS, D), 1.0, 6.0, ((0, 8), (1, 4)))
    cotangent = bell_draw(arg_keys[1], (TOKENS, D), 0.5, 3.0, ((0, 8), (1, 4)))
    route_ids_keys = jax.random.split(jax.random.fold_in(arg_keys[2], 1), TOKENS // TOK_DEV)
    route_ids_turns = jax.random.permutation(jax.random.fold_in(arg_keys[2], 3), TOKENS // TOK_DEV)
    route_ids = jax.vmap(lambda own, number: assign_block(jax.random.fold_in(arg_keys[2], 2), own, number, TOK_DEV, E, 2, CAP, 2))(route_ids_keys, route_ids_turns).reshape((TOKENS, 2))
    route_weights = jnp.clip(0.099609375 + 0.9003906 * jax.random.uniform(arg_keys[3], (TOKENS, 2), jnp.float32) ** steps_of(arg_keys[3], (TOKENS, 2), ((0, 8),), -0.2, 0.2), 0.099609375, 1.0).astype(jnp.bfloat16)
    reset_steps = touch_ends(jax.random.randint(arg_keys[4], (TOKENS // RB,), 0, STEPS), jax.random.fold_in(arg_keys[4], 1), 0, STEPS - 1).astype(jnp.int32)
    decay = jnp.clip(jnp.exp(math.log(0.9) - 1.50407736 * jax.random.uniform(arg_keys[5], (E, FF), jnp.float32) ** steps_of(arg_keys[5], (E, FF), ((0, 8), (1, 4)), -0.2, 0.2)), 0.2, 0.9)
    w_up = noise_with(arg_keys[6], (E, D, FF), D ** -0.5, 0.15625, ((0, 8), (2, 4)), (2, 1, 4, 2.0))
    w_down = bell_draw(arg_keys[7], (E, FF, D), FF ** -0.5, 0.125, ((0, 8), (1, 4)))
    return dict(tokens=tokens, cotangent=cotangent, route_ids=route_ids, route_weights=route_weights, reset_steps=reset_steps, decay=decay, w_up=w_up, w_down=w_down)


SHARP = 4.0

def lif_rates(current, decay, resets):
    membrane = jnp.zeros_like(current)
    rate_sum = jnp.zeros_like(current)
    for step_index in range(STEPS):
        keep_mask = (resets != step_index).astype(current.dtype)[:, None]
        membrane = keep_mask * decay[None, :] * membrane + current
        spike_now = jax.nn.sigmoid(SHARP * (membrane - 1.0))
        membrane = membrane - spike_now
        rate_sum = rate_sum + spike_now
    return rate_sum / STEPS

def reference(tokens, cotangent, route_ids, route_weights, reset_steps, decay, w_up, w_down):
    token_count = tokens.shape[0]
    experts = w_up.shape[0]
    slot_rows = N_SEQ * CAP
    block_units = FF // N_GRP
    pair_expert = route_ids.reshape(-1).astype(jnp.int32)
    pair_ids = jnp.arange(2 * token_count, dtype=jnp.int32)
    onehot = (pair_expert[:, None] == jnp.arange(experts, dtype=jnp.int32)[None, :]).astype(jnp.int32)
    position = lax.optimization_barrier(jnp.sum((jnp.cumsum(onehot, 0) - onehot) * onehot, 1)).astype(jnp.int32)
    table = jnp.full((experts, slot_rows), -1, jnp.int32).at[pair_expert, position].set(pair_ids)
    valid = table >= 0
    chosen = jnp.maximum(table, 0).astype(jnp.int32)
    token_reset = jnp.repeat(reset_steps, RB)
    gate_flat = route_weights.reshape(-1).astype(jnp.float32)

    def per_expert(expert):
        selected = chosen[expert]
        live = valid[expert]
        token_rows = selected // 2
        live_low = live.astype(jnp.bfloat16)[:, None]
        panel_x = tokens[token_rows] * live_low
        panel_dy = cotangent[token_rows] * live_low
        gate_values = gate_flat[selected] * live.astype(jnp.float32)
        resets = token_reset[token_rows]
        up_weight = w_up[expert]
        down_weight = w_down[expert]
        current = jnp.dot(panel_x, up_weight, preferred_element_type=jnp.float32)
        back_raw = jnp.dot(panel_dy, down_weight.T, preferred_element_type=jnp.float32)
        rate_values, pullback = jax.vjp(lambda drive: lif_rates(drive, decay[expert], resets), current)
        rates_low = rate_values.astype(jnp.bfloat16)
        gate_part = lax.optimization_barrier(jnp.sum(rates_low.astype(jnp.float32) * back_raw, 1))
        weighted = (rates_low.astype(jnp.float32) * gate_values[:, None]).astype(jnp.bfloat16)
        grad_down = jnp.dot(weighted.T, panel_dy, preferred_element_type=jnp.float32).astype(jnp.bfloat16)
        d_current = pullback(back_raw * gate_values[:, None])[0]
        d_low = d_current.astype(jnp.bfloat16)
        grad_up = jnp.dot(panel_x.T, d_low, preferred_element_type=jnp.float32).astype(jnp.bfloat16)
        blocks = jnp.einsum('mgf,dgf->gmd', d_low.reshape(slot_rows, N_GRP, block_units).astype(jnp.float32), up_weight.reshape(D, N_GRP, block_units).astype(jnp.float32)).astype(jnp.bfloat16)
        blocks = lax.optimization_barrier(blocks)
        input_rows = lax.optimization_barrier(jnp.sum(blocks.astype(jnp.float32), 0))
        return (grad_up, grad_down, input_rows, gate_part)
    grad_up, grad_down, input_rows, gate_rows = lax.map(per_expert, jnp.arange(experts, dtype=jnp.int32))
    flat_selected = chosen.reshape(-1)
    flat_live = valid.reshape(-1).astype(jnp.float32)
    grad_x = jnp.zeros((token_count, D), jnp.float32).at[flat_selected // 2].add(input_rows.reshape(-1, D) * flat_live[:, None]).astype(jnp.bfloat16)
    grad_route = jnp.zeros((2 * token_count,), jnp.float32).at[flat_selected].add(gate_rows.reshape(-1) * flat_live).reshape(token_count, 2)
    return (grad_x, grad_route, grad_up, grad_down)
```

```python
import functools

import jax
import jax.numpy as jnp
from jax import lax
from jax.experimental import pallas as pl
from jax.experimental.pallas import tpu as pltpu
from jax.sharding import PartitionSpec as P

STEPS = 4
RB = 16


SHARP = 4.0


def lif_rates(current, decay, resets):
    membrane = jnp.zeros_like(current)
    rate_sum = jnp.zeros_like(current)
    for step_index in range(STEPS):
        keep_mask = (resets != step_index).astype(jnp.float32)[:, None]
        membrane = keep_mask * decay[None, :] * membrane + current
        spike_now = jax.nn.sigmoid(SHARP * (membrane - 1.0))
        membrane = membrane - spike_now
        rate_sum = rate_sum + spike_now
    return rate_sum / STEPS


def plain_body(tokens, cotangent, route_ids, route_weights, reset_steps, decay, w_up, w_down):
    token_count = tokens.shape[0]
    feat_cols = tokens.shape[1]
    experts = lax.axis_size("seq")
    full_width = feat_cols * lax.axis_size("grp")
    capacity = 3 * token_count // experts
    slot_count = experts * capacity
    pair_expert = route_ids.reshape(-1)
    pair_ids = jnp.arange(2 * token_count, dtype=jnp.int32)
    onehot = (pair_expert[:, None] == jnp.arange(experts, dtype=jnp.int32)[None, :]).astype(
        jnp.int32
    )
    before = jnp.tril(jnp.ones((2 * token_count, 2 * token_count), jnp.bfloat16), -1)
    counts = jnp.dot(before, onehot.astype(jnp.bfloat16), preferred_element_type=jnp.float32)
    position = jnp.sum(counts.astype(jnp.int32) * onehot, 1)
    slot_of_pair = pair_expert * capacity + position
    pair_of_slot = jnp.zeros((slot_count,), jnp.int32).at[slot_of_pair].set(pair_ids)
    filled = jnp.zeros((slot_count,), jnp.bfloat16).at[slot_of_pair].set(1)
    token_of_slot = pair_of_slot // 2
    slot_mask = filled[:, None]
    gate_slot = (route_weights.reshape(-1)[pair_of_slot] * filled).reshape(experts, capacity)
    reset_slot = (
        jnp.repeat(reset_steps, RB)[token_of_slot].astype(jnp.bfloat16).reshape(experts, capacity)
    )
    whole_x, whole_dy = (
        lax.all_gather(tokens, "grp", axis=1, tiled=True),
        lax.all_gather(cotangent, "grp", axis=1, tiled=True),
    )
    send_x = (whole_x[token_of_slot] * slot_mask).reshape(experts, capacity, full_width)
    send_dy = (whole_dy[token_of_slot] * slot_mask).reshape(experts, capacity, full_width)
    panel_x, panel_dy, slot_gates, slot_resets = (
        lax.all_to_all(send_x, "seq", split_axis=0, concat_axis=0, tiled=True),
        lax.all_to_all(send_dy, "seq", split_axis=0, concat_axis=0, tiled=True),
        lax.all_to_all(gate_slot, "seq", split_axis=0, concat_axis=0, tiled=True),
        lax.all_to_all(reset_slot, "seq", split_axis=0, concat_axis=0, tiled=True),
    )
    panel_x = panel_x.reshape(slot_count, full_width)
    panel_dy = panel_dy.reshape(slot_count, full_width)
    gate_values = slot_gates.reshape(-1).astype(jnp.float32)
    resets = slot_resets.reshape(-1).astype(jnp.float32)
    up_local = w_up[0]
    down_local = w_down[0]
    decay_local = decay[0]
    current = jnp.dot(panel_x, up_local, preferred_element_type=jnp.float32)
    back_raw = lax.dot_general(
        panel_dy, down_local, (((1,), (1,)), ((), ())), preferred_element_type=jnp.float32
    )
    rate_values, pullback = jax.vjp(lambda drive: lif_rates(drive, decay_local, resets), current)
    rates_low = rate_values.astype(jnp.bfloat16)
    gate_part = jnp.sum(rates_low.astype(jnp.float32) * back_raw, 1)
    weighted = (rates_low.astype(jnp.float32) * gate_values[:, None]).astype(jnp.bfloat16)
    grad_down = lax.dot_general(
        weighted, panel_dy, (((0,), (0,)), ((), ())), preferred_element_type=jnp.float32
    ).astype(jnp.bfloat16)
    d_current = pullback(back_raw * gate_values[:, None])[0]
    d_low = d_current.astype(jnp.bfloat16)
    grad_up = lax.dot_general(
        panel_x, d_low, (((0,), (0,)), ((), ())), preferred_element_type=jnp.float32
    ).astype(jnp.bfloat16)
    input_rows = lax.psum_scatter(
        lax.dot_general(
            up_local, d_low, (((1,), (1,)), ((), ())), preferred_element_type=jnp.float32
        ).astype(jnp.bfloat16),
        "grp",
        scatter_dimension=0,
        tiled=True,
    ).astype(jnp.float32)
    gate_total = lax.psum(gate_part, "grp")
    back_x, back_gate = (
        lax.all_to_all(
            input_rows.reshape(feat_cols, experts, capacity).astype(jnp.bfloat16),
            "seq",
            split_axis=1,
            concat_axis=1,
            tiled=True,
        ).astype(jnp.float32),
        lax.all_to_all(
            gate_total.reshape(1, experts, capacity).astype(jnp.bfloat16),
            "seq",
            split_axis=1,
            concat_axis=1,
            tiled=True,
        ).astype(jnp.float32),
    )
    picked = back_x.reshape(feat_cols, slot_count)[:, slot_of_pair].reshape(
        feat_cols, token_count, 2
    )
    grad_x = jnp.sum(picked, 2).T.astype(jnp.bfloat16)
    grad_route = back_gate.reshape(-1)[slot_of_pair].reshape(token_count, 2)
    return (grad_x, grad_route, grad_up[None], grad_down[None])


MESH = pl.DeviceIdType.MESH
F32 = jnp.float32
BF16 = jnp.bfloat16


def flip(index, other, count):
    total, bit = 0, 1
    while bit < count:
        total = total + bit * ((index // bit + other // bit) % 2)
        bit *= 2
    return total


def nt_dot(a, b):
    return lax.dot_general(a, b, (((1,), (1,)), ((), ())), preferred_element_type=F32)


def tn_dot(a, b):
    return lax.dot_general(a, b, (((0,), (0,)), ((), ())), preferred_element_type=F32)


def moe_kernel(
    n_grp, n_seq,
    tok, cot, info, slot_cols, decay, up_hbm, down_hbm,
    gx_out, gr_out, gu_out, gd_out,
    up, down, zbuf, gmat, gmat_t, send, recv, msend, mrecv, cur, raw, wgt, dlow,
    rsend, rrecv, gsend, grecv, zsend, zrecv, own, row_send, row_recv, gu, gd,
    zs, zr, ds, dr, ms, mr, rs, rr, gs, gr, zbs, zbr, rws, rwr, local,
):
    z = lax.axis_index("grp")
    s = lax.axis_index("seq")
    tokens, width = tok.shape
    cap = recv.shape[3]
    slots = n_seq * cap
    hidden = up.shape[1]

    def z_copy(source, target, send_sem, recv_sem, o):
        return pltpu.make_async_remote_copy(
            src_ref=source, dst_ref=target, send_sem=send_sem, recv_sem=recv_sem,
            device_id=(flip(z, o, n_grp), s), device_id_type=MESH)

    def s_copy(source, target, send_sem, recv_sem, o):
        return pltpu.make_async_remote_copy(
            src_ref=source, dst_ref=target, send_sem=send_sem, recv_sem=recv_sem,
            device_id=(z, flip(s, o, n_seq)), device_id_type=MESH)

    load_up = pltpu.make_async_copy(up_hbm, up, local.at[0])
    load_down = pltpu.make_async_copy(down_hbm, down, local.at[1])
    load_up.start()
    load_down.start()

    barrier = pltpu.get_barrier_semaphore()
    for o in range(1, n_grp):
        pl.semaphore_signal(barrier, inc=1, device_id=(flip(z, o, n_grp), s), device_id_type=MESH)
    for o in range(1, n_seq):
        pl.semaphore_signal(barrier, inc=1, device_id=(z, flip(s, o, n_seq)), device_id_type=MESH)
    pl.semaphore_wait(barrier, n_grp + n_seq - 2)

    x_copies, y_copies = [None], [None]
    for o in range(1, n_grp):
        x_copies.append(z_copy(tok, zbuf.at[o, 0], zs.at[o, 0], zr.at[o, 0], o))
        y_copies.append(z_copy(cot, zbuf.at[o, 1], zs.at[o, 1], zr.at[o, 1], o))
        x_copies[o].start()
        y_copies[o].start()

    lane = lax.broadcasted_iota(jnp.int32, (cap, 128), 1)
    row_id = lax.broadcasted_iota(jnp.int32, (cap, tokens), 0)

    def hits(o):
        ids = (row_id + o * cap).astype(F32)
        return ids == info[0:1, :], ids == info[1:2, :]

    def prepare(o, carry):
        first, second = hits(o)
        either = jnp.where(first, 1.0, jnp.where(second, 1.0, 0.0))
        gmat[o] = either.astype(BF16)
        gate = jnp.sum(
            jnp.where(first, info[2:3, :], jnp.where(second, info[3:4, :], 0.0)), 1, keepdims=True)
        reset = jnp.sum(either * info[4:5, :], 1, keepdims=True)
        msend[o] = jnp.where(lane == 0, gate, reset)
        return carry

    lax.fori_loop(0, n_seq, prepare, 0)

    def dispatch(stage, x_ref, y_ref):
        def one(o, carry):
            send[stage, o, 0] = jnp.dot(
                gmat[o], x_ref[...], preferred_element_type=F32).astype(BF16)
            send[stage, o, 1] = jnp.dot(
                gmat[o], y_ref[...], preferred_element_type=F32).astype(BF16)
            s_copy(send.at[stage, o], recv.at[stage, o], ds.at[stage, o], dr.at[stage, o], o).start()
            return carry

        lax.fori_loop(1, n_seq, one, 0)
        recv[stage, 0, 0] = jnp.dot(gmat[0], x_ref[...], preferred_element_type=F32).astype(BF16)
        recv[stage, 0, 1] = jnp.dot(gmat[0], y_ref[...], preferred_element_type=F32).astype(BF16)

    dispatch(0, tok, cot)
    for o in range(1, n_seq):
        s_copy(msend.at[o], mrecv.at[o], ms.at[o], mr.at[o], o).start()
    mrecv[0] = msend[0]
    col_id = lax.broadcasted_iota(jnp.int32, (tokens, slots), 1).astype(F32)
    gmat_t[...] = jnp.where(
        col_id == slot_cols[:, 0:1], 1.0, jnp.where(col_id == slot_cols[:, 1:2], 1.0, 0.0)
    ).astype(BF16)
    for o in range(1, n_grp):
        x_copies[o].wait_recv()
        y_copies[o].wait_recv()
        dispatch(o, zbuf.at[o, 0], zbuf.at[o, 1])

    load_up.wait()
    load_down.wait()
    cur[...] = jnp.zeros_like(cur)
    raw[...] = jnp.zeros_like(raw)
    tile = min(hidden, 256)

    def slice_at(stage):
        return pl.multiple_of(flip(z, stage, n_grp) * width, width)

    def forward(stage, carry):
        def arrive(o, inner):
            s_copy(send.at[stage, o], recv.at[stage, o], ds.at[stage, o], dr.at[stage, o], o).wait_recv()
            return inner

        lax.fori_loop(1, n_seq, arrive, 0)
        base = slice_at(stage)

        def columns(n, inner):
            at = pl.multiple_of(n * tile, tile)
            x = recv[stage, :, 0].reshape(slots, width)
            cur[:, pl.ds(at, tile)] += jnp.dot(
                x, up[pl.ds(base, width), pl.ds(at, tile)], preferred_element_type=F32)
            y = recv[stage, :, 1].reshape(slots, width)
            raw[:, pl.ds(at, tile)] += nt_dot(y, down[pl.ds(at, tile), pl.ds(base, width)])
            return inner

        lax.fori_loop(0, hidden // tile, columns, 0)
        return carry

    lax.fori_loop(0, n_grp, forward, 0)
    for o in range(1, n_seq):
        s_copy(msend.at[o], mrecv.at[o], ms.at[o], mr.at[o], o).wait_recv()

    rows = 16

    def neurons(o, carry):
        def part(i, inner):
            at = pl.multiple_of(o * cap + i * rows, rows)
            here = pl.multiple_of(i * rows, rows)
            drive = cur[pl.ds(at, rows), :]
            back = raw[pl.ds(at, rows), :]
            gate = mrecv[o, pl.ds(here, rows), 0:1]
            reset = mrecv[o, pl.ds(here, rows), 1:2]
            leak = decay[0:1, :]
            spikes, scales = [], []
            membrane = None
            for step in range(STEPS):
                if step == 0:
                    membrane = drive
                    scales.append(None)
                else:
                    keep = jnp.where(reset == float(step), 0.0, 1.0)
                    scale = keep * leak
                    scales.append(scale)
                    membrane = scale * membrane + drive
                spike = jax.nn.sigmoid(SHARP * (membrane - 1.0))
                membrane = membrane - spike
                spikes.append(spike)
            rate = ((spikes[0] + spikes[1] + spikes[2] + spikes[3]) / STEPS).astype(BF16).astype(F32)
            total = jnp.sum(rate * back, 1, keepdims=True)
            gsend[o, pl.ds(here, rows), :] = jnp.broadcast_to(total, (rows, 128))
            wgt[pl.ds(at, rows), :] = (rate * gate).astype(BF16)
            upstream = back * gate / STEPS
            d_v, d_cur = None, None
            for step in reversed(range(STEPS)):
                spike = spikes[step]
                slope = SHARP * spike * (1.0 - spike)
                if d_v is None:
                    d_m = upstream * slope
                    d_cur = d_m
                else:
                    d_m = d_v + (upstream - d_v) * slope
                    d_cur = d_cur + d_m
                if step > 0:
                    d_v = scales[step] * d_m
            dlow[pl.ds(at, rows), :] = d_cur.astype(BF16)
            return inner

        lax.fori_loop(0, cap // rows, part, 0)
        return carry

    lax.fori_loop(0, n_seq, neurons, 0)

    for o in range(1, n_seq):
        s_copy(gsend.at[o], grecv.at[o], gs.at[o], gr.at[o], o).start()
    grecv[0] = gsend[0]

    half = n_seq // 2

    def give_back(turn, carry):
        stage = n_grp - 1 - turn
        base = slice_at(stage)

        def block(h, inner):
            at = pl.multiple_of(h * half * cap, half * cap)
            value = nt_dot(dlow[pl.ds(at, half * cap), :], up[pl.ds(base, width), :]).astype(BF16)
            rsend[stage, pl.ds(h * half, half)] = value.reshape(half, cap, width)
            return inner

        lax.fori_loop(0, 2, block, 0)
        rrecv[stage, 0] = rsend[stage, 0]

        def go(o, inner):
            s_copy(rsend.at[stage, o], rrecv.at[stage, o], rs.at[stage, o], rr.at[stage, o], o).start()
            return inner

        lax.fori_loop(1, n_seq, go, 0)
        return carry

    lax.fori_loop(0, n_grp, give_back, 0)

    def weight_grads(stage, carry):
        base = slice_at(stage)
        gu[pl.ds(base, width), :] = tn_dot(
            recv[stage, :, 0].reshape(slots, width), dlow[...]).astype(BF16)
        gd[:, pl.ds(base, width)] = tn_dot(
            wgt[...], recv[stage, :, 1].reshape(slots, width)).astype(BF16)
        return carry

    lax.fori_loop(0, n_grp, weight_grads, 0)
    store_up = pltpu.make_async_copy(gu, gu_out, local.at[2])
    store_down = pltpu.make_async_copy(gd, gd_out, local.at[3])
    store_up.start()
    store_down.start()

    for o in range(1, n_seq):
        s_copy(gsend.at[o], grecv.at[o], gs.at[o], gr.at[o], o).wait_recv()

    def route(o, carry):
        first, second = hits(o)
        gates = jnp.concatenate([grecv[o]] * (tokens // 128), axis=1)
        return (
            carry[0] + jnp.sum(jnp.where(first, gates, 0.0), 0, keepdims=True),
            carry[1] + jnp.sum(jnp.where(second, gates, 0.0), 0, keepdims=True),
        )

    empty = jnp.zeros((1, tokens), F32)
    route0, route1 = lax.fori_loop(0, n_seq, route, (empty, empty))
    which = lax.broadcasted_iota(jnp.int32, (8, tokens), 0)
    row_send[...] = jnp.where(which == 0, route0, route1)
    row_copies = [None] + [
        z_copy(row_send, row_recv.at[o], rws.at[o], rwr.at[o], o) for o in range(1, n_grp)]
    for o in range(1, n_grp):
        row_copies[o].start()

    x_back = [None] + [
        z_copy(zsend.at[o], zrecv.at[o], zbs.at[o], zbr.at[o], o) for o in range(1, n_grp)]
    for stage in reversed(range(n_grp)):
        for o in range(1, n_seq):
            s_copy(rsend.at[stage, o], rrecv.at[stage, o], rs.at[stage, o], rr.at[stage, o], o).wait_recv()
        value = jnp.dot(
            gmat_t[...], rrecv[stage].reshape(slots, width), preferred_element_type=F32)
        if stage > 0:
            zsend[stage] = value.astype(BF16)
            x_back[stage].start()
        else:
            own[...] = value
    total_rows = row_send[...]
    for o in range(1, n_grp):
        row_copies[o].wait_recv()
        total_rows = total_rows + row_recv[o]
    gr_out[...] = total_rows
    for o in reversed(range(1, n_grp)):
        x_back[o].wait_recv()
        own[...] += zrecv[o].astype(F32)
    gx_out[...] = own[...].astype(BF16)

    for o in range(1, n_grp):
        x_copies[o].wait_send()
        y_copies[o].wait_send()
        row_copies[o].wait_send()
        x_back[o].wait_send()

    def finish(o, carry):
        s_copy(msend.at[o], mrecv.at[o], ms.at[o], mr.at[o], o).wait_send()
        s_copy(gsend.at[o], grecv.at[o], gs.at[o], gr.at[o], o).wait_send()

        def each(stage, inner):
            s_copy(send.at[stage, o], recv.at[stage, o], ds.at[stage, o], dr.at[stage, o], o).wait_send()
            s_copy(rsend.at[stage, o], rrecv.at[stage, o], rs.at[stage, o], rr.at[stage, o], o).wait_send()
            return inner

        lax.fori_loop(0, n_grp, each, 0)
        return carry

    lax.fori_loop(1, n_seq, finish, 0)
    store_up.wait()
    store_down.wait()


def body(tokens, cotangent, route_ids, route_weights, reset_steps, decay, w_up, w_down):
    token_count, width = tokens.shape
    n_grp, n_seq = lax.axis_size("grp"), lax.axis_size("seq")
    cap = 3 * token_count // n_seq
    slots = n_seq * cap
    _, full, hidden = w_up.shape
    if width % 128 or cap % 16 or hidden % 256 or token_count % 128 or n_grp & (n_grp - 1) or n_seq & (n_seq - 1):
        return plain_body(
            tokens, cotangent, route_ids, route_weights, reset_steps, decay, w_up, w_down)
    experts = jnp.arange(n_seq, dtype=jnp.int32)
    onehot = (route_ids[:, :, None] == experts[None, None, :]).astype(F32)
    both = jnp.sum(onehot, 1).astype(BF16)
    before = jnp.tril(jnp.ones((token_count, token_count), BF16), -1)
    counts = jnp.dot(before, both, preferred_element_type=F32)
    position = jnp.sum(counts[:, None, :] * onehot, 2)
    block = (route_ids ^ lax.axis_index("seq")).astype(F32)
    slot = block * cap + position
    resets = jnp.repeat(reset_steps, RB).astype(F32)
    info = jnp.concatenate(
        [slot.T, route_weights.astype(F32).T, resets[None], jnp.zeros((3, token_count), F32)], 0)
    slot_cols = slot
    vmem = pl.BlockSpec(memory_space=pltpu.VMEM)
    hbm = pl.BlockSpec(memory_space=pl.ANY)
    dma = pltpu.SemaphoreType.DMA
    panel = (n_grp, n_seq, cap, width)
    grad_x, rows, grad_up, grad_down = pl.pallas_call(
        functools.partial(moe_kernel, n_grp, n_seq),
        out_shape=(
            jax.ShapeDtypeStruct((token_count, width), BF16),
            jax.ShapeDtypeStruct((8, token_count), F32),
            jax.ShapeDtypeStruct((full, hidden), BF16),
            jax.ShapeDtypeStruct((hidden, full), BF16),
        ),
        in_specs=[vmem, vmem, vmem, vmem, vmem, hbm, hbm],
        out_specs=(vmem, vmem, hbm, hbm),
        scratch_shapes=[
            pltpu.VMEM((full, hidden), BF16),
            pltpu.VMEM((hidden, full), BF16),
            pltpu.VMEM((n_grp, 2, token_count, width), BF16),
            pltpu.VMEM((n_seq, cap, token_count), BF16),
            pltpu.VMEM((token_count, slots), BF16),
            pltpu.VMEM((n_grp, n_seq, 2, cap, width), BF16),
            pltpu.VMEM((n_grp, n_seq, 2, cap, width), BF16),
            pltpu.VMEM((n_seq, cap, 128), F32),
            pltpu.VMEM((n_seq, cap, 128), F32),
            pltpu.VMEM((slots, hidden), F32),
            pltpu.VMEM((slots, hidden), F32),
            pltpu.VMEM((slots, hidden), BF16),
            pltpu.VMEM((slots, hidden), BF16),
            pltpu.VMEM(panel, BF16),
            pltpu.VMEM(panel, BF16),
            pltpu.VMEM((n_seq, cap, 128), F32),
            pltpu.VMEM((n_seq, cap, 128), F32),
            pltpu.VMEM((n_grp, token_count, width), BF16),
            pltpu.VMEM((n_grp, token_count, width), BF16),
            pltpu.VMEM((token_count, width), F32),
            pltpu.VMEM((8, token_count), F32),
            pltpu.VMEM((n_grp, 8, token_count), F32),
            pltpu.VMEM((full, hidden), BF16),
            pltpu.VMEM((hidden, full), BF16),
            dma((n_grp, 2)), dma((n_grp, 2)),
            dma((n_grp, n_seq)), dma((n_grp, n_seq)),
            dma((n_seq,)), dma((n_seq,)),
            dma((n_grp, n_seq)), dma((n_grp, n_seq)),
            dma((n_seq,)), dma((n_seq,)),
            dma((n_grp,)), dma((n_grp,)),
            dma((n_grp,)), dma((n_grp,)),
            dma((4,)),
        ],
        compiler_params=pltpu.CompilerParams(
            collective_id=0, has_side_effects=True, vmem_limit_bytes=60 * 1024 * 1024),
    )(tokens, cotangent, info, slot_cols, decay, w_up[0], w_down[0])
    return grad_x, rows[:2].T, grad_up[None], grad_down[None]


def solution(mesh):
    in_specs = (
        P("seq", "grp"),
        P("seq", "grp"),
        P("seq", None),
        P("seq", None),
        P("seq"),
        P("seq", "grp"),
        P("seq", None, "grp"),
        P("seq", "grp", None),
    )
    out_specs = (P("seq", "grp"), P("seq", None), P("seq", None, "grp"), P("seq", "grp", None))
    return jax.shard_map(body, mesh=mesh, in_specs=in_specs, out_specs=out_specs, check_vma=False)
```

```python
import functools

import jax
import jax.numpy as jnp
from jax import lax
from jax.experimental import pallas as pl
from jax.experimental.pallas import tpu as pltpu
from jax.sharding import PartitionSpec as P

STEPS = 4
RB = 16


SHARP = 4.0


def lif_rates(current, decay, resets):
    membrane = jnp.zeros_like(current)
    rate_sum = jnp.zeros_like(current)
    for step_index in range(STEPS):
        keep_mask = (resets != step_index).astype(jnp.float32)[:, None]
        membrane = keep_mask * decay[None, :] * membrane + current
        spike_now = jax.nn.sigmoid(SHARP * (membrane - 1.0))
        membrane = membrane - spike_now
        rate_sum = rate_sum + spike_now
    return rate_sum / STEPS


def plain_body(tokens, cotangent, route_ids, route_weights, reset_steps, decay, w_up, w_down):
    token_count = tokens.shape[0]
    feat_cols = tokens.shape[1]
    experts = lax.axis_size("seq")
    full_width = feat_cols * lax.axis_size("grp")
    capacity = 3 * token_count // experts
    slot_count = experts * capacity
    pair_expert = route_ids.reshape(-1)
    pair_ids = jnp.arange(2 * token_count, dtype=jnp.int32)
    onehot = (pair_expert[:, None] == jnp.arange(experts, dtype=jnp.int32)[None, :]).astype(
        jnp.int32
    )
    before = jnp.tril(jnp.ones((2 * token_count, 2 * token_count), jnp.bfloat16), -1)
    counts = jnp.dot(before, onehot.astype(jnp.bfloat16), preferred_element_type=jnp.float32)
    position = jnp.sum(counts.astype(jnp.int32) * onehot, 1)
    slot_of_pair = pair_expert * capacity + position
    pair_of_slot = jnp.zeros((slot_count,), jnp.int32).at[slot_of_pair].set(pair_ids)
    filled = jnp.zeros((slot_count,), jnp.bfloat16).at[slot_of_pair].set(1)
    token_of_slot = pair_of_slot // 2
    slot_mask = filled[:, None]
    gate_slot = (route_weights.reshape(-1)[pair_of_slot] * filled).reshape(experts, capacity)
    reset_slot = (
        jnp.repeat(reset_steps, RB)[token_of_slot].astype(jnp.bfloat16).reshape(experts, capacity)
    )
    whole_x, whole_dy = (
        lax.all_gather(tokens, "grp", axis=1, tiled=True),
        lax.all_gather(cotangent, "grp", axis=1, tiled=True),
    )
    send_x = (whole_x[token_of_slot] * slot_mask).reshape(experts, capacity, full_width)
    send_dy = (whole_dy[token_of_slot] * slot_mask).reshape(experts, capacity, full_width)
    panel_x, panel_dy, slot_gates, slot_resets = (
        lax.all_to_all(send_x, "seq", split_axis=0, concat_axis=0, tiled=True),
        lax.all_to_all(send_dy, "seq", split_axis=0, concat_axis=0, tiled=True),
        lax.all_to_all(gate_slot, "seq", split_axis=0, concat_axis=0, tiled=True),
        lax.all_to_all(reset_slot, "seq", split_axis=0, concat_axis=0, tiled=True),
    )
    panel_x = panel_x.reshape(slot_count, full_width)
    panel_dy = panel_dy.reshape(slot_count, full_width)
    gate_values = slot_gates.reshape(-1).astype(jnp.float32)
    resets = slot_resets.reshape(-1).astype(jnp.float32)
    up_local = w_up[0]
    down_local = w_down[0]
    decay_local = decay[0]
    current = jnp.dot(panel_x, up_local, preferred_element_type=jnp.float32)
    back_raw = lax.dot_general(
        panel_dy, down_local, (((1,), (1,)), ((), ())), preferred_element_type=jnp.float32
    )
    rate_values, pullback = jax.vjp(lambda drive: lif_rates(drive, decay_local, resets), current)
    rates_low = rate_values.astype(jnp.bfloat16)
    gate_part = jnp.sum(rates_low.astype(jnp.float32) * back_raw, 1)
    weighted = (rates_low.astype(jnp.float32) * gate_values[:, None]).astype(jnp.bfloat16)
    grad_down = lax.dot_general(
        weighted, panel_dy, (((0,), (0,)), ((), ())), preferred_element_type=jnp.float32
    ).astype(jnp.bfloat16)
    d_current = pullback(back_raw * gate_values[:, None])[0]
    d_low = d_current.astype(jnp.bfloat16)
    grad_up = lax.dot_general(
        panel_x, d_low, (((0,), (0,)), ((), ())), preferred_element_type=jnp.float32
    ).astype(jnp.bfloat16)
    input_rows = lax.psum_scatter(
        lax.dot_general(
            up_local, d_low, (((1,), (1,)), ((), ())), preferred_element_type=jnp.float32
        ).astype(jnp.bfloat16),
        "grp",
        scatter_dimension=0,
        tiled=True,
    ).astype(jnp.float32)
    gate_total = lax.psum(gate_part, "grp")
    back_x, back_gate = (
        lax.all_to_all(
            input_rows.reshape(feat_cols, experts, capacity).astype(jnp.bfloat16),
            "seq",
            split_axis=1,
            concat_axis=1,
            tiled=True,
        ).astype(jnp.float32),
        lax.all_to_all(
            gate_total.reshape(1, experts, capacity).astype(jnp.bfloat16),
            "seq",
            split_axis=1,
            concat_axis=1,
            tiled=True,
        ).astype(jnp.float32),
    )
    picked = back_x.reshape(feat_cols, slot_count)[:, slot_of_pair].reshape(
        feat_cols, token_count, 2
    )
    grad_x = jnp.sum(picked, 2).T.astype(jnp.bfloat16)
    grad_route = back_gate.reshape(-1)[slot_of_pair].reshape(token_count, 2)
    return (grad_x, grad_route, grad_up[None], grad_down[None])


MESH = pl.DeviceIdType.MESH
F32 = jnp.float32
BF16 = jnp.bfloat16


def flip(index, other, count):
    total, bit = 0, 1
    while bit < count:
        total = total + bit * ((index // bit + other // bit) % 2)
        bit *= 2
    return total


def nt_dot(a, b):
    return lax.dot_general(a, b, (((1,), (1,)), ((), ())), preferred_element_type=F32)


def tn_dot(a, b):
    return lax.dot_general(a, b, (((0,), (0,)), ((), ())), preferred_element_type=F32)


def moe_kernel(
    n_grp, n_seq,
    tok, cot, info, slot_cols, decay, up_hbm, down_hbm,
    gx_out, gr_out, gu_out, gd_out,
    up, down, zbuf, gmat, gmat_t, send, recv, msend, mrecv, cur, raw, wgt, dlow,
    rsend, rrecv, gsend, grecv, zsend, zrecv, own, row_send, row_recv, gu, gd,
    zs, zr, ds, dr, ms, mr, rs, rr, gs, gr, zbs, zbr, rws, rwr, fs, fr, es, er, local,
):
    z = lax.axis_index("grp")
    s = lax.axis_index("seq")
    tokens, width = tok.shape
    cap = recv.shape[3]
    slots = n_seq * cap
    hidden = up.shape[1]

    def z_copy(source, target, send_sem, recv_sem, o):
        return pltpu.make_async_remote_copy(
            src_ref=source, dst_ref=target, send_sem=send_sem, recv_sem=recv_sem,
            device_id=(flip(z, o, n_grp), s), device_id_type=MESH)

    def s_copy(source, target, send_sem, recv_sem, o):
        return pltpu.make_async_remote_copy(
            src_ref=source, dst_ref=target, send_sem=send_sem, recv_sem=recv_sem,
            device_id=(z, flip(s, o, n_seq)), device_id_type=MESH)

    load_up = pltpu.make_async_copy(up_hbm, up, local.at[0])
    load_down = pltpu.make_async_copy(down_hbm, down, local.at[1])
    load_up.start()
    load_down.start()

    barrier = pltpu.get_barrier_semaphore()
    for o in range(1, n_grp):
        pl.semaphore_signal(barrier, inc=1, device_id=(flip(z, o, n_grp), s), device_id_type=MESH)
    for o in range(1, n_seq):
        pl.semaphore_signal(barrier, inc=1, device_id=(z, flip(s, o, n_seq)), device_id_type=MESH)
    pl.semaphore_wait(barrier, n_grp + n_seq - 2)

    far = [
        z_copy(tok, zbuf.at[2, 0], zs.at[2, 0], zr.at[2, 0], 2),
        z_copy(cot, zbuf.at[2, 1], zs.at[2, 1], zr.at[2, 1], 2),
    ]
    relay = [z_copy(zbuf.at[2, a], zbuf.at[3, a], zs.at[3, a], zr.at[3, a], 1) for a in (0, 1)]
    for copy in far:
        copy.start()

    lane = lax.broadcasted_iota(jnp.int32, (cap, 128), 1)
    row_id = lax.broadcasted_iota(jnp.int32, (cap, tokens), 0)

    def hits(o):
        ids = (row_id + o * cap).astype(F32)
        return ids == info[0:1, :], ids == info[1:2, :]

    def prepare(o, carry):
        first, second = hits(o)
        either = jnp.where(first, 1.0, jnp.where(second, 1.0, 0.0))
        gmat[o] = either.astype(BF16)
        gate = jnp.sum(
            jnp.where(first, info[2:3, :], jnp.where(second, info[3:4, :], 0.0)), 1, keepdims=True)
        reset = jnp.sum(either * info[4:5, :], 1, keepdims=True)
        msend[o] = jnp.where(lane == 0, gate, reset)
        return carry

    lax.fori_loop(0, n_seq, prepare, 0)

    def dispatch(stage, x_ref, y_ref):
        def one(o, carry):
            send[stage, o, 0] = jnp.dot(
                gmat[o], x_ref[...], preferred_element_type=F32).astype(BF16)
            send[stage, o, 1] = jnp.dot(
                gmat[o], y_ref[...], preferred_element_type=F32).astype(BF16)
            s_copy(send.at[stage, o], recv.at[stage, o], ds.at[stage, o], dr.at[stage, o], o).start()
            return carry

        lax.fori_loop(1, n_seq, one, 0)
        recv[stage, 0, 0] = jnp.dot(gmat[0], x_ref[...], preferred_element_type=F32).astype(BF16)
        recv[stage, 0, 1] = jnp.dot(gmat[0], y_ref[...], preferred_element_type=F32).astype(BF16)

    dispatch(0, tok, cot)
    for o in range(1, n_seq):
        s_copy(msend.at[o], mrecv.at[o], ms.at[o], mr.at[o], o).start()
    mrecv[0] = msend[0]
    col_id = lax.broadcasted_iota(jnp.int32, (tokens, slots), 1).astype(F32)
    gmat_t[...] = jnp.where(
        col_id == slot_cols[:, 0:1], 1.0, jnp.where(col_id == slot_cols[:, 1:2], 1.0, 0.0)
    ).astype(BF16)

    def pass_panel(o):
        return z_copy(recv.at[0, o], recv.at[1, o], fs.at[o], fr.at[o], 1)

    def pass_on(o, carry):
        s_copy(send.at[0, o], recv.at[0, o], ds.at[0, o], dr.at[0, o], o).wait_recv()
        pass_panel(o).start()
        return carry

    pass_panel(0).start()
    lax.fori_loop(1, n_seq // 2, pass_on, 0)
    for copy, onward in zip(far, relay):
        copy.wait_recv()
        onward.start()
    dispatch(2, zbuf.at[2, 0], zbuf.at[2, 1])
    lax.fori_loop(n_seq // 2, n_seq, pass_on, 0)
    for onward in relay:
        onward.wait_recv()
    dispatch(3, zbuf.at[3, 0], zbuf.at[3, 1])

    load_up.wait()
    load_down.wait()
    cur[...] = jnp.zeros_like(cur)
    raw[...] = jnp.zeros_like(raw)
    tile = min(hidden, 256)

    def slice_at(stage):
        return pl.multiple_of(flip(z, stage, n_grp) * width, width)

    def forward(stage):
        def arrive(o, inner):
            if stage == 1:
                pass_panel(o).wait_recv()
            else:
                s_copy(
                    send.at[stage, o], recv.at[stage, o], ds.at[stage, o], dr.at[stage, o], o
                ).wait_recv()
            return inner

        if stage > 0:
            lax.fori_loop(0 if stage == 1 else 1, n_seq, arrive, 0)
        base = slice_at(stage)

        def columns(n, inner):
            at = pl.multiple_of(n * tile, tile)
            x = recv[stage, :, 0].reshape(slots, width)
            cur[:, pl.ds(at, tile)] += jnp.dot(
                x, up[pl.ds(base, width), pl.ds(at, tile)], preferred_element_type=F32)
            y = recv[stage, :, 1].reshape(slots, width)
            raw[:, pl.ds(at, tile)] += nt_dot(y, down[pl.ds(at, tile), pl.ds(base, width)])
            return inner

        lax.fori_loop(0, hidden // tile, columns, 0)

    for stage in (0, 2, 1, 3):
        forward(stage)
    for o in range(1, n_seq):
        s_copy(msend.at[o], mrecv.at[o], ms.at[o], mr.at[o], o).wait_recv()

    rows = 16

    def neurons(o, carry):
        def part(i, inner):
            at = pl.multiple_of(o * cap + i * rows, rows)
            here = pl.multiple_of(i * rows, rows)
            drive = cur[pl.ds(at, rows), :]
            back = raw[pl.ds(at, rows), :]
            gate = mrecv[o, pl.ds(here, rows), 0:1]
            reset = mrecv[o, pl.ds(here, rows), 1:2]
            leak = decay[0:1, :]
            spikes, scales = [], []
            membrane = None
            for step in range(STEPS):
                if step == 0:
                    membrane = drive
                    scales.append(None)
                else:
                    keep = jnp.where(reset == float(step), 0.0, 1.0)
                    scale = keep * leak
                    scales.append(scale)
                    membrane = scale * membrane + drive
                spike = jax.nn.sigmoid(SHARP * (membrane - 1.0))
                membrane = membrane - spike
                spikes.append(spike)
            rate = ((spikes[0] + spikes[1] + spikes[2] + spikes[3]) / STEPS).astype(BF16).astype(F32)
            total = jnp.sum(rate * back, 1, keepdims=True)
            gsend[o, pl.ds(here, rows), :] = jnp.broadcast_to(total, (rows, 128))
            wgt[pl.ds(at, rows), :] = (rate * gate).astype(BF16)
            upstream = back * gate / STEPS
            d_v, d_cur = None, None
            for step in reversed(range(STEPS)):
                spike = spikes[step]
                slope = SHARP * spike * (1.0 - spike)
                if d_v is None:
                    d_m = upstream * slope
                    d_cur = d_m
                else:
                    d_m = d_v + (upstream - d_v) * slope
                    d_cur = d_cur + d_m
                if step > 0:
                    d_v = scales[step] * d_m
            dlow[pl.ds(at, rows), :] = d_cur.astype(BF16)
            return inner

        lax.fori_loop(0, cap // rows, part, 0)
        return carry

    lax.fori_loop(0, n_seq, neurons, 0)

    for o in range(1, n_seq):
        s_copy(gsend.at[o], grecv.at[o], gs.at[o], gr.at[o], o).start()
    grecv[0] = gsend[0]

    half = n_seq // 2

    def to_partner(h):
        part = pl.ds(h * half, half)
        return z_copy(rsend.at[1, part], rrecv.at[1, part], es.at[h], er.at[h], 1)

    def give_back(stage):
        base = slice_at(stage)

        def block(h, inner):
            at = pl.multiple_of(h * half * cap, half * cap)
            value = nt_dot(dlow[pl.ds(at, half * cap), :], up[pl.ds(base, width), :])
            value = value.reshape(half, cap, width)
            if stage == 0:
                to_partner(h).wait_recv()
                value = value + rrecv[1, pl.ds(h * half, half)].astype(F32)
            rsend[stage, pl.ds(h * half, half)] = value.astype(BF16)
            if stage == 1:
                to_partner(h).start()
            return inner

        def go(o, inner):
            s_copy(rsend.at[stage, o], rrecv.at[stage, o], rs.at[stage, o], rr.at[stage, o], o).start()
            return inner

        lax.fori_loop(0, 2, block, 0)
        if stage != 1:
            rrecv[stage, 0] = rsend[stage, 0]
            lax.fori_loop(1, n_seq, go, 0)

    for stage in (1, 3, 2):
        give_back(stage)

    def weight_grads(stage, carry):
        base = slice_at(stage)
        gu[pl.ds(base, width), :] = tn_dot(
            recv[stage, :, 0].reshape(slots, width), dlow[...]).astype(BF16)
        gd[:, pl.ds(base, width)] = tn_dot(
            wgt[...], recv[stage, :, 1].reshape(slots, width)).astype(BF16)
        return carry

    lax.fori_loop(0, n_grp, weight_grads, 0)
    give_back(0)
    store_up = pltpu.make_async_copy(gu, gu_out, local.at[2])
    store_down = pltpu.make_async_copy(gd, gd_out, local.at[3])
    store_up.start()
    store_down.start()

    for o in range(1, n_seq):
        s_copy(gsend.at[o], grecv.at[o], gs.at[o], gr.at[o], o).wait_recv()

    def route(o, carry):
        first, second = hits(o)
        gates = jnp.concatenate([grecv[o]] * (tokens // 128), axis=1)
        return (
            carry[0] + jnp.sum(jnp.where(first, gates, 0.0), 0, keepdims=True),
            carry[1] + jnp.sum(jnp.where(second, gates, 0.0), 0, keepdims=True),
        )

    empty = jnp.zeros((1, tokens), F32)
    route0, route1 = lax.fori_loop(0, n_seq, route, (empty, empty))
    which = lax.broadcasted_iota(jnp.int32, (8, tokens), 0)
    row_send[...] = jnp.where(which == 0, route0, route1)
    row_copies = [None] + [
        z_copy(row_send, row_recv.at[o], rws.at[o], rwr.at[o], o) for o in range(1, n_grp)]
    for o in range(1, n_grp):
        row_copies[o].start()

    x_back = {o: z_copy(zsend.at[o], zrecv.at[o], zbs.at[o], zbr.at[o], o) for o in (2, 3)}
    for stage in (3, 2, 0):
        for o in range(1, n_seq):
            s_copy(rsend.at[stage, o], rrecv.at[stage, o], rs.at[stage, o], rr.at[stage, o], o).wait_recv()
        value = jnp.dot(
            gmat_t[...], rrecv[stage].reshape(slots, width), preferred_element_type=F32)
        if stage > 0:
            zsend[stage] = value.astype(BF16)
            x_back[stage].start()
        else:
            own[...] = value
    total_rows = row_send[...]
    for o in range(1, n_grp):
        row_copies[o].wait_recv()
        total_rows = total_rows + row_recv[o]
    gr_out[...] = total_rows
    for o in (3, 2):
        x_back[o].wait_recv()
        own[...] += zrecv[o].astype(F32)
    gx_out[...] = own[...].astype(BF16)

    for copy in far + relay + [x_back[2], x_back[3]] + row_copies[1:]:
        copy.wait_send()
    for h in (0, 1):
        to_partner(h).wait_send()
    pass_panel(0).wait_send()

    def finish(o, carry):
        s_copy(msend.at[o], mrecv.at[o], ms.at[o], mr.at[o], o).wait_send()
        s_copy(gsend.at[o], grecv.at[o], gs.at[o], gr.at[o], o).wait_send()

        pass_panel(o).wait_send()

        def each(turn, inner):
            stage = turn + (turn + 2) // 3
            s_copy(send.at[stage, o], recv.at[stage, o], ds.at[stage, o], dr.at[stage, o], o).wait_send()
            s_copy(rsend.at[stage, o], rrecv.at[stage, o], rs.at[stage, o], rr.at[stage, o], o).wait_send()
            return inner

        lax.fori_loop(0, 3, each, 0)
        return carry

    lax.fori_loop(1, n_seq, finish, 0)
    store_up.wait()
    store_down.wait()


def body(tokens, cotangent, route_ids, route_weights, reset_steps, decay, w_up, w_down):
    token_count, width = tokens.shape
    n_grp, n_seq = lax.axis_size("grp"), lax.axis_size("seq")
    cap = 3 * token_count // n_seq
    slots = n_seq * cap
    _, full, hidden = w_up.shape
    if width % 128 or cap % 16 or hidden % 256 or token_count % 128 or n_grp != 4 or n_seq & (n_seq - 1):
        return plain_body(
            tokens, cotangent, route_ids, route_weights, reset_steps, decay, w_up, w_down)
    experts = jnp.arange(n_seq, dtype=jnp.int32)
    onehot = (route_ids[:, :, None] == experts[None, None, :]).astype(F32)
    both = jnp.sum(onehot, 1).astype(BF16)
    before = jnp.tril(jnp.ones((token_count, token_count), BF16), -1)
    counts = jnp.dot(before, both, preferred_element_type=F32)
    position = jnp.sum(counts[:, None, :] * onehot, 2)
    block = (route_ids ^ lax.axis_index("seq")).astype(F32)
    slot = block * cap + position
    resets = jnp.repeat(reset_steps, RB).astype(F32)
    info = jnp.concatenate(
        [slot.T, route_weights.astype(F32).T, resets[None], jnp.zeros((3, token_count), F32)], 0)
    slot_cols = slot
    vmem = pl.BlockSpec(memory_space=pltpu.VMEM)
    hbm = pl.BlockSpec(memory_space=pl.ANY)
    dma = pltpu.SemaphoreType.DMA
    panel = (n_grp, n_seq, cap, width)
    grad_x, rows, grad_up, grad_down = pl.pallas_call(
        functools.partial(moe_kernel, n_grp, n_seq),
        out_shape=(
            jax.ShapeDtypeStruct((token_count, width), BF16),
            jax.ShapeDtypeStruct((8, token_count), F32),
            jax.ShapeDtypeStruct((full, hidden), BF16),
            jax.ShapeDtypeStruct((hidden, full), BF16),
        ),
        in_specs=[vmem, vmem, vmem, vmem, vmem, hbm, hbm],
        out_specs=(vmem, vmem, hbm, hbm),
        scratch_shapes=[
            pltpu.VMEM((full, hidden), BF16),
            pltpu.VMEM((hidden, full), BF16),
            pltpu.VMEM((n_grp, 2, token_count, width), BF16),
            pltpu.VMEM((n_seq, cap, token_count), BF16),
            pltpu.VMEM((token_count, slots), BF16),
            pltpu.VMEM((n_grp, n_seq, 2, cap, width), BF16),
            pltpu.VMEM((n_grp, n_seq, 2, cap, width), BF16),
            pltpu.VMEM((n_seq, cap, 128), F32),
            pltpu.VMEM((n_seq, cap, 128), F32),
            pltpu.VMEM((slots, hidden), F32),
            pltpu.VMEM((slots, hidden), F32),
            pltpu.VMEM((slots, hidden), BF16),
            pltpu.VMEM((slots, hidden), BF16),
            pltpu.VMEM(panel, BF16),
            pltpu.VMEM(panel, BF16),
            pltpu.VMEM((n_seq, cap, 128), F32),
            pltpu.VMEM((n_seq, cap, 128), F32),
            pltpu.VMEM((n_grp, token_count, width), BF16),
            pltpu.VMEM((n_grp, token_count, width), BF16),
            pltpu.VMEM((token_count, width), F32),
            pltpu.VMEM((8, token_count), F32),
            pltpu.VMEM((n_grp, 8, token_count), F32),
            pltpu.VMEM((full, hidden), BF16),
            pltpu.VMEM((hidden, full), BF16),
            dma((n_grp, 2)), dma((n_grp, 2)),
            dma((n_grp, n_seq)), dma((n_grp, n_seq)),
            dma((n_seq,)), dma((n_seq,)),
            dma((n_grp, n_seq)), dma((n_grp, n_seq)),
            dma((n_seq,)), dma((n_seq,)),
            dma((n_grp,)), dma((n_grp,)),
            dma((n_grp,)), dma((n_grp,)),
            dma((n_seq,)), dma((n_seq,)),
            dma((2,)), dma((2,)),
            dma((4,)),
        ],
        compiler_params=pltpu.CompilerParams(
            collective_id=0, has_side_effects=True, vmem_limit_bytes=60 * 1024 * 1024),
    )(tokens, cotangent, info, slot_cols, decay, w_up[0], w_down[0])
    return grad_x, rows[:2].T, grad_up[None], grad_down[None]


def solution(mesh):
    in_specs = (
        P("seq", "grp"),
        P("seq", "grp"),
        P("seq", None),
        P("seq", None),
        P("seq"),
        P("seq", "grp"),
        P("seq", None, "grp"),
        P("seq", "grp", None),
    )
    out_specs = (P("seq", "grp"), P("seq", None), P("seq", None, "grp"), P("seq", "grp", None))
    return jax.shard_map(body, mesh=mesh, in_specs=in_specs, out_specs=out_specs, check_vma=False)
```

```python
import functools

import jax
import jax.numpy as jnp
from jax import lax
from jax.experimental import pallas as pl
from jax.experimental.pallas import tpu as pltpu
from jax.sharding import PartitionSpec as P

STEPS = 4
RB = 16


SHARP = 4.0


def lif_rates(current, decay, resets):
    membrane = jnp.zeros_like(current)
    rate_sum = jnp.zeros_like(current)
    for step_index in range(STEPS):
        keep_mask = (resets != step_index).astype(jnp.float32)[:, None]
        membrane = keep_mask * decay[None, :] * membrane + current
        spike_now = jax.nn.sigmoid(SHARP * (membrane - 1.0))
        membrane = membrane - spike_now
        rate_sum = rate_sum + spike_now
    return rate_sum / STEPS


def plain_body(tokens, cotangent, route_ids, route_weights, reset_steps, decay, w_up, w_down):
    token_count = tokens.shape[0]
    feat_cols = tokens.shape[1]
    experts = lax.axis_size("seq")
    full_width = feat_cols * lax.axis_size("grp")
    capacity = 3 * token_count // experts
    slot_count = experts * capacity
    pair_expert = route_ids.reshape(-1)
    pair_ids = jnp.arange(2 * token_count, dtype=jnp.int32)
    onehot = (pair_expert[:, None] == jnp.arange(experts, dtype=jnp.int32)[None, :]).astype(
        jnp.int32
    )
    before = jnp.tril(jnp.ones((2 * token_count, 2 * token_count), jnp.bfloat16), -1)
    counts = jnp.dot(before, onehot.astype(jnp.bfloat16), preferred_element_type=jnp.float32)
    position = jnp.sum(counts.astype(jnp.int32) * onehot, 1)
    slot_of_pair = pair_expert * capacity + position
    pair_of_slot = jnp.zeros((slot_count,), jnp.int32).at[slot_of_pair].set(pair_ids)
    filled = jnp.zeros((slot_count,), jnp.bfloat16).at[slot_of_pair].set(1)
    token_of_slot = pair_of_slot // 2
    slot_mask = filled[:, None]
    gate_slot = (route_weights.reshape(-1)[pair_of_slot] * filled).reshape(experts, capacity)
    reset_slot = (
        jnp.repeat(reset_steps, RB)[token_of_slot].astype(jnp.bfloat16).reshape(experts, capacity)
    )
    whole_x, whole_dy = (
        lax.all_gather(tokens, "grp", axis=1, tiled=True),
        lax.all_gather(cotangent, "grp", axis=1, tiled=True),
    )
    send_x = (whole_x[token_of_slot] * slot_mask).reshape(experts, capacity, full_width)
    send_dy = (whole_dy[token_of_slot] * slot_mask).reshape(experts, capacity, full_width)
    panel_x, panel_dy, slot_gates, slot_resets = (
        lax.all_to_all(send_x, "seq", split_axis=0, concat_axis=0, tiled=True),
        lax.all_to_all(send_dy, "seq", split_axis=0, concat_axis=0, tiled=True),
        lax.all_to_all(gate_slot, "seq", split_axis=0, concat_axis=0, tiled=True),
        lax.all_to_all(reset_slot, "seq", split_axis=0, concat_axis=0, tiled=True),
    )
    panel_x = panel_x.reshape(slot_count, full_width)
    panel_dy = panel_dy.reshape(slot_count, full_width)
    gate_values = slot_gates.reshape(-1).astype(jnp.float32)
    resets = slot_resets.reshape(-1).astype(jnp.float32)
    up_local = w_up[0]
    down_local = w_down[0]
    decay_local = decay[0]
    current = jnp.dot(panel_x, up_local, preferred_element_type=jnp.float32)
    back_raw = lax.dot_general(
        panel_dy, down_local, (((1,), (1,)), ((), ())), preferred_element_type=jnp.float32
    )
    rate_values, pullback = jax.vjp(lambda drive: lif_rates(drive, decay_local, resets), current)
    rates_low = rate_values.astype(jnp.bfloat16)
    gate_part = jnp.sum(rates_low.astype(jnp.float32) * back_raw, 1)
    weighted = (rates_low.astype(jnp.float32) * gate_values[:, None]).astype(jnp.bfloat16)
    grad_down = lax.dot_general(
        weighted, panel_dy, (((0,), (0,)), ((), ())), preferred_element_type=jnp.float32
    ).astype(jnp.bfloat16)
    d_current = pullback(back_raw * gate_values[:, None])[0]
    d_low = d_current.astype(jnp.bfloat16)
    grad_up = lax.dot_general(
        panel_x, d_low, (((0,), (0,)), ((), ())), preferred_element_type=jnp.float32
    ).astype(jnp.bfloat16)
    input_rows = lax.psum_scatter(
        lax.dot_general(
            up_local, d_low, (((1,), (1,)), ((), ())), preferred_element_type=jnp.float32
        ).astype(jnp.bfloat16),
        "grp",
        scatter_dimension=0,
        tiled=True,
    ).astype(jnp.float32)
    gate_total = lax.psum(gate_part, "grp")
    back_x, back_gate = (
        lax.all_to_all(
            input_rows.reshape(feat_cols, experts, capacity).astype(jnp.bfloat16),
            "seq",
            split_axis=1,
            concat_axis=1,
            tiled=True,
        ).astype(jnp.float32),
        lax.all_to_all(
            gate_total.reshape(1, experts, capacity).astype(jnp.bfloat16),
            "seq",
            split_axis=1,
            concat_axis=1,
            tiled=True,
        ).astype(jnp.float32),
    )
    picked = back_x.reshape(feat_cols, slot_count)[:, slot_of_pair].reshape(
        feat_cols, token_count, 2
    )
    grad_x = jnp.sum(picked, 2).T.astype(jnp.bfloat16)
    grad_route = back_gate.reshape(-1)[slot_of_pair].reshape(token_count, 2)
    return (grad_x, grad_route, grad_up[None], grad_down[None])


MESH = pl.DeviceIdType.MESH
F32 = jnp.float32
BF16 = jnp.bfloat16


def flip(index, other, count):
    total, bit = 0, 1
    while bit < count:
        total = total + bit * ((index // bit + other // bit) % 2)
        bit *= 2
    return total


def nt_dot(a, b):
    return lax.dot_general(a, b, (((1,), (1,)), ((), ())), preferred_element_type=F32)


def tn_dot(a, b):
    return lax.dot_general(a, b, (((0,), (0,)), ((), ())), preferred_element_type=F32)


def moe_kernel(
    n_grp, n_seq,
    tok, cot, info, slot_cols, decay, up_hbm, down_hbm,
    gx_out, gr_out, gu_out, gd_out,
    up, down, zbuf, gmat, gmat_t, send, recv, msend, mrecv, cur, raw, wgt, dlow,
    rsend, rrecv, gsend, grecv, zsend, zrecv, own, row_send, row_recv, gu, gd,
    zs, zr, ds, dr, ms, mr, rs, rr, gs, gr, zbs, zbr, rws, rwr, fs, fr, es, er, local,
):
    z = lax.axis_index("grp")
    s = lax.axis_index("seq")
    tokens, width = tok.shape
    cap = recv.shape[3]
    slots = n_seq * cap
    hidden = up.shape[1]

    def z_copy(source, target, send_sem, recv_sem, o):
        return pltpu.make_async_remote_copy(
            src_ref=source, dst_ref=target, send_sem=send_sem, recv_sem=recv_sem,
            device_id=(flip(z, o, n_grp), s), device_id_type=MESH)

    def s_copy(source, target, send_sem, recv_sem, o):
        return pltpu.make_async_remote_copy(
            src_ref=source, dst_ref=target, send_sem=send_sem, recv_sem=recv_sem,
            device_id=(z, flip(s, o, n_seq)), device_id_type=MESH)

    load_up = pltpu.make_async_copy(up_hbm, up, local.at[0])
    load_down = pltpu.make_async_copy(down_hbm, down, local.at[1])
    load_up.start()
    load_down.start()

    barrier = pltpu.get_barrier_semaphore()
    for o in range(1, n_grp):
        pl.semaphore_signal(barrier, inc=1, device_id=(flip(z, o, n_grp), s), device_id_type=MESH)
    for o in range(1, n_seq):
        pl.semaphore_signal(barrier, inc=1, device_id=(z, flip(s, o, n_seq)), device_id_type=MESH)
    pl.semaphore_wait(barrier, n_grp + n_seq - 2)

    far = [
        z_copy(tok, zbuf.at[2, 0], zs.at[2, 0], zr.at[2, 0], 2),
        z_copy(cot, zbuf.at[2, 1], zs.at[2, 1], zr.at[2, 1], 2),
    ]
    relay = [z_copy(zbuf.at[2, a], zbuf.at[3, a], zs.at[3, a], zr.at[3, a], 1) for a in (0, 1)]
    for copy in far:
        copy.start()

    lane = lax.broadcasted_iota(jnp.int32, (cap, 128), 1)
    row_id = lax.broadcasted_iota(jnp.int32, (cap, tokens), 0)

    def hits(o):
        ids = (row_id + o * cap).astype(F32)
        return ids == info[0:1, :], ids == info[1:2, :]

    def prepare(o, carry):
        first, second = hits(o)
        either = jnp.where(first, 1.0, jnp.where(second, 1.0, 0.0))
        gmat[o] = either.astype(BF16)
        gate = jnp.sum(
            jnp.where(first, info[2:3, :], jnp.where(second, info[3:4, :], 0.0)), 1, keepdims=True)
        reset = jnp.sum(either * info[4:5, :], 1, keepdims=True)
        msend[o] = jnp.where(lane == 0, gate, reset)
        return carry

    lax.fori_loop(0, n_seq, prepare, 0)

    def dispatch(stage, x_ref, y_ref):
        def one(o, carry):
            send[stage, o, 0] = jnp.dot(
                gmat[o], x_ref[...], preferred_element_type=F32).astype(BF16)
            send[stage, o, 1] = jnp.dot(
                gmat[o], y_ref[...], preferred_element_type=F32).astype(BF16)
            s_copy(send.at[stage, o], recv.at[stage, o], ds.at[stage, o], dr.at[stage, o], o).start()
            return carry

        lax.fori_loop(1, n_seq, one, 0)
        recv[stage, 0, 0] = jnp.dot(gmat[0], x_ref[...], preferred_element_type=F32).astype(BF16)
        recv[stage, 0, 1] = jnp.dot(gmat[0], y_ref[...], preferred_element_type=F32).astype(BF16)

    dispatch(0, tok, cot)
    for o in range(1, n_seq):
        s_copy(msend.at[o], mrecv.at[o], ms.at[o], mr.at[o], o).start()
    mrecv[0] = msend[0]
    col_id = lax.broadcasted_iota(jnp.int32, (tokens, slots), 1).astype(F32)
    gmat_t[...] = jnp.where(
        col_id == slot_cols[:, 0:1], 1.0, jnp.where(col_id == slot_cols[:, 1:2], 1.0, 0.0)
    ).astype(BF16)

    def pass_panel(o):
        return z_copy(recv.at[0, o], recv.at[1, o], fs.at[o], fr.at[o], 1)

    def pass_on(o, carry):
        s_copy(send.at[0, o], recv.at[0, o], ds.at[0, o], dr.at[0, o], o).wait_recv()
        pass_panel(o).start()
        return carry

    pass_panel(0).start()
    lax.fori_loop(1, n_seq // 2, pass_on, 0)
    for copy, onward in zip(far, relay):
        copy.wait_recv()
        onward.start()
    dispatch(2, zbuf.at[2, 0], zbuf.at[2, 1])
    lax.fori_loop(n_seq // 2, n_seq, pass_on, 0)
    for onward in relay:
        onward.wait_recv()
    dispatch(3, zbuf.at[3, 0], zbuf.at[3, 1])

    load_up.wait()
    load_down.wait()
    cur[...] = jnp.zeros_like(cur)
    raw[...] = jnp.zeros_like(raw)
    tile = min(hidden, 256)

    def slice_at(stage):
        return pl.multiple_of(flip(z, stage, n_grp) * width, width)

    def forward(stage):
        def arrive(o, inner):
            if stage == 1:
                pass_panel(o).wait_recv()
            else:
                s_copy(
                    send.at[stage, o], recv.at[stage, o], ds.at[stage, o], dr.at[stage, o], o
                ).wait_recv()
            return inner

        if stage > 0:
            lax.fori_loop(0 if stage == 1 else 1, n_seq, arrive, 0)
        base = slice_at(stage)

        def columns(n, inner):
            at = pl.multiple_of(n * tile, tile)
            x = recv[stage, :, 0].reshape(slots, width)
            cur[:, pl.ds(at, tile)] += jnp.dot(
                x, up[pl.ds(base, width), pl.ds(at, tile)], preferred_element_type=F32)
            y = recv[stage, :, 1].reshape(slots, width)
            raw[:, pl.ds(at, tile)] += nt_dot(y, down[pl.ds(at, tile), pl.ds(base, width)])
            return inner

        lax.fori_loop(0, hidden // tile, columns, 0)

    for stage in (0, 2, 1, 3):
        forward(stage)
    for o in range(1, n_seq):
        s_copy(msend.at[o], mrecv.at[o], ms.at[o], mr.at[o], o).wait_recv()

    rows = 32 if cap % 32 == 0 else 16

    def neurons(o, carry):
        def part(i, inner):
            at = pl.multiple_of(o * cap + i * rows, rows)
            here = pl.multiple_of(i * rows, rows)
            drive = cur[pl.ds(at, rows), :]
            back = raw[pl.ds(at, rows), :]
            gate = mrecv[o, pl.ds(here, rows), 0:1]
            reset = mrecv[o, pl.ds(here, rows), 1:2]
            leak = decay[0:1, :]
            waves, scales, spikes = [], [], None
            membrane = None
            for step in range(STEPS):
                if step == 0:
                    membrane = drive
                    scales.append(None)
                else:
                    keep = jnp.where(reset == float(step), 0.0, 1.0)
                    scale = keep * leak
                    scales.append(scale)
                    membrane = scale * membrane + drive
                wave = jnp.tanh(0.5 * SHARP * (membrane - 1.0))
                spike = 0.5 + 0.5 * wave
                membrane = membrane - spike
                waves.append(wave)
                spikes = spike if spikes is None else spikes + spike
            rate = (spikes * (1.0 / STEPS)).astype(BF16).astype(F32)
            total = jnp.sum(rate * back, 1, keepdims=True)
            gsend[o, pl.ds(here, rows), :] = jnp.broadcast_to(total, (rows, 128))
            wgt[pl.ds(at, rows), :] = (rate * gate).astype(BF16)
            upstream = back * gate * (1.0 / STEPS)
            d_v, d_cur = None, None
            for step in reversed(range(STEPS)):
                slope = (0.25 * SHARP) * (1.0 - waves[step] * waves[step])
                if d_v is None:
                    d_m = upstream * slope
                    d_cur = d_m
                else:
                    d_m = d_v + (upstream - d_v) * slope
                    d_cur = d_cur + d_m
                if step > 0:
                    d_v = scales[step] * d_m
            dlow[pl.ds(at, rows), :] = d_cur.astype(BF16)
            return inner

        lax.fori_loop(0, cap // rows, part, 0)
        return carry

    half = n_seq // 2

    def to_partner(h):
        part = pl.ds(h * half, half)
        return z_copy(rsend.at[1, part], rrecv.at[1, part], es.at[h], er.at[h], 1)

    def give_back(stage, h):
        base = slice_at(stage)
        value = nt_dot(
            dlow[h * half * cap:(h + 1) * half * cap, :], up[pl.ds(base, width), :])
        value = value.reshape(half, cap, width)
        if stage == 0:
            to_partner(h).wait_recv()
            value = value + rrecv[1, h * half:(h + 1) * half].astype(F32)
        rsend[stage, h * half:(h + 1) * half] = value.astype(BF16)

        def go(o, inner):
            s_copy(rsend.at[stage, o], rrecv.at[stage, o], rs.at[stage, o], rr.at[stage, o], o).start()
            return inner

        if stage == 1:
            to_partner(h).start()
        else:
            lax.fori_loop(max(1, h * half), (h + 1) * half, go, 0)
            if h == 0:
                rrecv[stage, 0] = rsend[stage, 0]

    for h in (0, 1):
        lax.fori_loop(h * half, (h + 1) * half, neurons, 0)
        for stage in (1, 3, 2):
            give_back(stage, h)
    for o in range(1, n_seq):
        s_copy(gsend.at[o], grecv.at[o], gs.at[o], gr.at[o], o).start()
    grecv[0] = gsend[0]

    def weight_grads(stage, carry):
        base = slice_at(stage)
        gu[pl.ds(base, width), :] = tn_dot(
            recv[stage, :, 0].reshape(slots, width), dlow[...]).astype(BF16)
        gd[:, pl.ds(base, width)] = tn_dot(
            wgt[...], recv[stage, :, 1].reshape(slots, width)).astype(BF16)
        return carry

    lax.fori_loop(0, n_grp, weight_grads, 0)
    give_back(0, 0)
    give_back(0, 1)
    store_up = pltpu.make_async_copy(gu, gu_out, local.at[2])
    store_down = pltpu.make_async_copy(gd, gd_out, local.at[3])
    store_up.start()
    store_down.start()

    for o in range(1, n_seq):
        s_copy(gsend.at[o], grecv.at[o], gs.at[o], gr.at[o], o).wait_recv()

    def route(o, carry):
        first, second = hits(o)
        gates = jnp.concatenate([grecv[o]] * (tokens // 128), axis=1)
        return (
            carry[0] + jnp.sum(jnp.where(first, gates, 0.0), 0, keepdims=True),
            carry[1] + jnp.sum(jnp.where(second, gates, 0.0), 0, keepdims=True),
        )

    empty = jnp.zeros((1, tokens), F32)
    route0, route1 = lax.fori_loop(0, n_seq, route, (empty, empty))
    which = lax.broadcasted_iota(jnp.int32, (8, tokens), 0)
    row_send[...] = jnp.where(which == 0, route0, route1)
    row_copies = [None] + [
        z_copy(row_send, row_recv.at[o], rws.at[o], rwr.at[o], o) for o in range(1, n_grp)]
    for o in range(1, n_grp):
        row_copies[o].start()

    x_back = {o: z_copy(zsend.at[o], zrecv.at[o], zbs.at[o], zbr.at[o], o) for o in (2, 3)}
    for stage in (3, 2, 0):
        for o in range(1, n_seq):
            s_copy(rsend.at[stage, o], rrecv.at[stage, o], rs.at[stage, o], rr.at[stage, o], o).wait_recv()
        value = jnp.dot(
            gmat_t[...], rrecv[stage].reshape(slots, width), preferred_element_type=F32)
        if stage > 0:
            zsend[stage] = value.astype(BF16)
            x_back[stage].start()
        else:
            own[...] = value
    total_rows = row_send[...]
    for o in range(1, n_grp):
        row_copies[o].wait_recv()
        total_rows = total_rows + row_recv[o]
    gr_out[...] = total_rows
    for o in (3, 2):
        x_back[o].wait_recv()
        own[...] += zrecv[o].astype(F32)
    gx_out[...] = own[...].astype(BF16)

    for copy in far + relay + [x_back[2], x_back[3]] + row_copies[1:]:
        copy.wait_send()
    for h in (0, 1):
        to_partner(h).wait_send()
    pass_panel(0).wait_send()

    def finish(o, carry):
        s_copy(msend.at[o], mrecv.at[o], ms.at[o], mr.at[o], o).wait_send()
        s_copy(gsend.at[o], grecv.at[o], gs.at[o], gr.at[o], o).wait_send()

        pass_panel(o).wait_send()

        def each(turn, inner):
            stage = turn + (turn + 2) // 3
            s_copy(send.at[stage, o], recv.at[stage, o], ds.at[stage, o], dr.at[stage, o], o).wait_send()
            s_copy(rsend.at[stage, o], rrecv.at[stage, o], rs.at[stage, o], rr.at[stage, o], o).wait_send()
            return inner

        lax.fori_loop(0, 3, each, 0)
        return carry

    lax.fori_loop(1, n_seq, finish, 0)
    store_up.wait()
    store_down.wait()


def body(tokens, cotangent, route_ids, route_weights, reset_steps, decay, w_up, w_down):
    token_count, width = tokens.shape
    n_grp, n_seq = lax.axis_size("grp"), lax.axis_size("seq")
    cap = 3 * token_count // n_seq
    slots = n_seq * cap
    _, full, hidden = w_up.shape
    if width % 128 or cap % 16 or hidden % 256 or token_count % 128 or n_grp != 4 or n_seq & (n_seq - 1):
        return plain_body(
            tokens, cotangent, route_ids, route_weights, reset_steps, decay, w_up, w_down)
    experts = jnp.arange(n_seq, dtype=jnp.int32)
    onehot = (route_ids[:, :, None] == experts[None, None, :]).astype(F32)
    both = jnp.sum(onehot, 1).astype(BF16)
    before = jnp.tril(jnp.ones((token_count, token_count), BF16), -1)
    counts = jnp.dot(before, both, preferred_element_type=F32)
    position = jnp.sum(counts[:, None, :] * onehot, 2)
    block = (route_ids ^ lax.axis_index("seq")).astype(F32)
    slot = block * cap + position
    resets = jnp.repeat(reset_steps, RB).astype(F32)
    info = jnp.concatenate(
        [slot.T, route_weights.astype(F32).T, resets[None], jnp.zeros((3, token_count), F32)], 0)
    slot_cols = slot
    vmem = pl.BlockSpec(memory_space=pltpu.VMEM)
    hbm = pl.BlockSpec(memory_space=pl.ANY)
    dma = pltpu.SemaphoreType.DMA
    panel = (n_grp, n_seq, cap, width)
    grad_x, rows, grad_up, grad_down = pl.pallas_call(
        functools.partial(moe_kernel, n_grp, n_seq),
        out_shape=(
            jax.ShapeDtypeStruct((token_count, width), BF16),
            jax.ShapeDtypeStruct((8, token_count), F32),
            jax.ShapeDtypeStruct((full, hidden), BF16),
            jax.ShapeDtypeStruct((hidden, full), BF16),
        ),
        in_specs=[vmem, vmem, vmem, vmem, vmem, hbm, hbm],
        out_specs=(vmem, vmem, hbm, hbm),
        scratch_shapes=[
            pltpu.VMEM((full, hidden), BF16),
            pltpu.VMEM((hidden, full), BF16),
            pltpu.VMEM((n_grp, 2, token_count, width), BF16),
            pltpu.VMEM((n_seq, cap, token_count), BF16),
            pltpu.VMEM((token_count, slots), BF16),
            pltpu.VMEM((n_grp, n_seq, 2, cap, width), BF16),
            pltpu.VMEM((n_grp, n_seq, 2, cap, width), BF16),
            pltpu.VMEM((n_seq, cap, 128), F32),
            pltpu.VMEM((n_seq, cap, 128), F32),
            pltpu.VMEM((slots, hidden), F32),
            pltpu.VMEM((slots, hidden), F32),
            pltpu.VMEM((slots, hidden), BF16),
            pltpu.VMEM((slots, hidden), BF16),
            pltpu.VMEM(panel, BF16),
            pltpu.VMEM(panel, BF16),
            pltpu.VMEM((n_seq, cap, 128), F32),
            pltpu.VMEM((n_seq, cap, 128), F32),
            pltpu.VMEM((n_grp, token_count, width), BF16),
            pltpu.VMEM((n_grp, token_count, width), BF16),
            pltpu.VMEM((token_count, width), F32),
            pltpu.VMEM((8, token_count), F32),
            pltpu.VMEM((n_grp, 8, token_count), F32),
            pltpu.VMEM((full, hidden), BF16),
            pltpu.VMEM((hidden, full), BF16),
            dma((n_grp, 2)), dma((n_grp, 2)),
            dma((n_grp, n_seq)), dma((n_grp, n_seq)),
            dma((n_seq,)), dma((n_seq,)),
            dma((n_grp, n_seq)), dma((n_grp, n_seq)),
            dma((n_seq,)), dma((n_seq,)),
            dma((n_grp,)), dma((n_grp,)),
            dma((n_grp,)), dma((n_grp,)),
            dma((n_seq,)), dma((n_seq,)),
            dma((2,)), dma((2,)),
            dma((4,)),
        ],
        compiler_params=pltpu.CompilerParams(
            collective_id=0, has_side_effects=True, vmem_limit_bytes=60 * 1024 * 1024),
    )(tokens, cotangent, info, slot_cols, decay, w_up[0], w_down[0])
    return grad_x, rows[:2].T, grad_up[None], grad_down[None]


def solution(mesh):
    in_specs = (
        P("seq", "grp"),
        P("seq", "grp"),
        P("seq", None),
        P("seq", None),
        P("seq"),
        P("seq", "grp"),
        P("seq", None, "grp"),
        P("seq", "grp", None),
    )
    out_specs = (P("seq", "grp"), P("seq", None), P("seq", None, "grp"), P("seq", "grp", None))
    return jax.shard_map(body, mesh=mesh, in_specs=in_specs, out_specs=out_specs, check_vma=False)
```
